512 devices in a mesh: seq: 64 (over y, z_hi, core), head: 8 (over x, z_lo).
Axes of the slice: x: 4, y: 8, z: 8 (z_hi: 4, z_lo: 2; z = z_hi * 2 + z_lo), core: 2. Of those that a mesh axis runs over, the one named last changes fastest.
Arguments:
- query_rows: bfloat16 [32768, 4096], P(('seq', 'head')), may hold values from -18 to 18
- key_rows: bfloat16 [32768, 4096], P(('seq', 'head')), may hold values from -18 to 18
- value_rows: bfloat16 [32768, 4096], P(('seq', 'head')), may hold values from -6 to 6
- doc_first: int32 [64], replicated, may hold values from 0 to 63, as said below
Outputs:
- attended: bfloat16 [32768, 4096], P(('seq', 'head'))
- log_totals: float32 [32, 32768], P('head', 'seq')
The draws below stay inside these ranges and needn't reach their ends.
Inputs may be any that keep to these rules, and one draw needn't show every extreme that they name: The blocks form documents of consecutive blocks: doc_first never falls, doc_first[doc_first[b]] = doc_first[b], b - 8 < doc_first[b] <= b, and some document holds exactly 8 blocks.
All inputs are finite; a program needn't handle non-finite values.
Results may differ from the reference program's by a relative error of at most 0.0059.
Values may be sent and summed in bfloat16 or wider, within the bound.
A program may use at most 64 MiB of HBM per device.

```python
import math
import jax
import jax.numpy as jnp
from jax import lax

HEADS = 32
HD = 128
TOK_DEV = 512
D = 4096
TOKENS = 32768
REACH = 8
N_SEQ = 64


def draw_query_rows(key, part):
    key = jax.random.fold_in(key, 3)
    sample = jnp.clip(jax.random.normal(key, (TOKENS, D), jnp.float32), -6.0, 6.0)
    return sample.astype(jnp.bfloat16)


def draw_key_rows(key, part):
    key = jax.random.fold_in(key, 5)
    sample = jnp.clip(jax.random.normal(key, (TOKENS, D), jnp.float32), -6.0, 6.0)
    return sample.astype(jnp.bfloat16)


def draw_doc_first(key, part):
    key = jax.random.fold_in(key, 7)
    lengths = jax.random.randint(key, (N_SEQ,), 1, REACH + 1)
    longest = jax.random.randint(jax.random.fold_in(key, 1), (), 0, 3)
    blocks = jnp.arange(N_SEQ)
    lengths = jnp.where(blocks == longest, REACH, lengths)
    starts = jnp.cumsum(lengths) - lengths
    found = jnp.where(starts[None, :] <= blocks[:, None], starts[None, :], 0)
    return jnp.max(found, axis=1).astype(jnp.int32)


def levels(rng, extent, shards, least, top_value):
    level, own = 1.0, jax.random.fold_in(rng, 6)
    for axis_at, parts in shards:
        steps = jnp.exp(jax.random.uniform(jax.random.fold_in(own, axis_at), (parts,), jnp.float32, least / len(shards), top_value / len(shards)))
        level = level * jnp.repeat(steps, extent[axis_at] // parts).reshape([-1 if axis == axis_at else 1 for axis in range(len(extent))])
    return level


def centred(rng, dims, scale, most, split=(), kind=jnp.bfloat16):
    drawn = scale * jax.random.normal(rng, dims, jnp.float32)
    if split:
        drawn = drawn * levels(rng, dims, split, -0.22, 0.18)
    return jnp.clip(drawn, -most, most).astype(kind)


def setup_inputs(seed: int = 0) -> dict:
    streams_of = jax.random.split(jax.random.key(seed), 5)
    return {
        "query_rows": draw_query_rows(jax.random.fold_in(streams_of[4], 71), 0),
        "key_rows": draw_key_rows(jax.random.fold_in(streams_of[4], 71), 0),
        "value_rows": centred(streams_of[2], (TOKENS, D), 1.0, 6.0, ((0, 512),)),
        "doc_first": draw_doc_first(jax.random.fold_in(streams_of[4], 71), 0),
    }


def attend_tile(queries, key_block, value_block, causal):
    scaling = 1.0 / math.sqrt(HD)
    scores = jnp.einsum('qhd,khd->hqk', queries.astype(jnp.float32), key_block.astype(jnp.float32), precision=lax.Precision.HIGHEST) * scaling
    if causal is not None:
        scores = jnp.where(causal[None], scores, -jnp.inf)
    maxima = lax.optimization_barrier(jnp.max(scores, axis=-1))
    weights = jnp.exp(scores - maxima[..., None]).astype(jnp.bfloat16)
    totals = lax.optimization_barrier(jnp.sum(weights.astype(jnp.float32), axis=-1))
    partial_value = jnp.einsum('hqk,khd->hqd', weights.astype(jnp.float32), value_block.astype(jnp.float32), precision=lax.Precision.HIGHEST)
    return (maxima, totals, partial_value)

def combine(running, fresh):
    highest = jnp.maximum(running[0], fresh[0])
    old_scale = jnp.exp(running[0] - highest)
    new_scale = jnp.exp(fresh[0] - highest)
    return (highest, running[1] * old_scale + fresh[1] * new_scale, running[2] * old_scale[..., None] + fresh[2] * new_scale[..., None])

def reference(query_rows, key_rows, value_rows, doc_first):
    query_blocks = query_rows.reshape(N_SEQ, TOK_DEV, HEADS, HD)
    key_blocks = key_rows.reshape(N_SEQ, TOK_DEV, HEADS, HD)
    value_blocks = value_rows.reshape(N_SEQ, TOK_DEV, HEADS, HD)
    indices = jnp.arange(TOK_DEV, dtype=jnp.int32)
    causal = indices[:, None] >= indices[None, :]

    def one_block(target):
        queries = query_blocks[target]
        backward = target - doc_first[target]
        running = attend_tile(queries, key_blocks[target], value_blocks[target], causal)
        for step_index in range(1, REACH):
            source = jnp.maximum(target - step_index, 0).astype(jnp.int32)

            def with_tile(held, source=source):
                return combine(held, attend_tile(queries, key_blocks[source], value_blocks[source], None))

            def without_tile(held):
                return held
            running = lax.cond(step_index <= backward, with_tile, without_tile, running)
        maxima, totals, partial_value = running
        output = (partial_value / totals[..., None]).transpose(1, 0, 2).reshape(TOK_DEV, HEADS * HD)
        return (output.astype(jnp.bfloat16), maxima + jnp.log(totals))
    outputs, log_blocks = lax.map(one_block, jnp.arange(N_SEQ, dtype=jnp.int32))
    attended = outputs.reshape(TOKENS, D)
    log_totals = log_blocks.transpose(1, 0, 2).reshape(HEADS, TOKENS)
    return (attended, log_totals)
```

```python
import functools
import math

import jax
import jax.numpy as jnp
from jax import lax
from jax.experimental import pallas as pl
from jax.experimental.pallas import tpu as pltpu
from jax.sharding import PartitionSpec as P

HD = 128
NX, NY, NZ = 4, 8, 8
PLANE = NX * NZ
ROWS = 64
BLOCK = 512
SUBS = BLOCK // ROWS
NB = 8
OWN = NB // 2
SCALE = 1.0 / math.sqrt(HD)
FLAGS = {"kv": True, "q": True, "fwd": True, "compute": True, "out": True}


def chip_device(y, x, z, core):
    return ((y * 4 + z // 2) * 2 + core, x * 2 + z % 2)


def shift(t):
    turn = t // 4
    far = 4 - (turn + 1) // 2
    dz = (8 + far * (2 * (turn % 2) - 1)) % 8
    return 3 - t % 4, dz


def attend_kernel(
    doc_ref, q_ref, k_ref, v_ref, out_ref, lse_ref,
    qbuf, kv, obuf, scores, lse_stage, lse_in,
    kv_send, kv_recv, q_send, q_recv, sib_send, sib_recv, fwd_send, fwd_recv,
    prev_send, prev_recv, o_send, o_recv, lse_send, lse_recv, local_sem,
):
    seq = lax.axis_index("seq")
    head = lax.axis_index("head")
    core = seq % 2
    y = seq // 8
    x = head // 2
    z = (seq // 2) % 4 * 2 + head % 2
    my_block = seq % 8
    my_sub = head
    my_head = x * 8 + z

    sibling = chip_device(y, x, z, 1 - core)
    ahead = chip_device((y + 1) % NY, x, z, core)
    behind = chip_device((y + NY - 1) % NY, x, z, core)

    def target(t):
        dx, dz = shift(t)
        tx, tz = (x + dx) % NX, (z + dz) % NZ
        return chip_device(y, tx, tz, core), tx * 8 + tz

    def source(t):
        dx, dz = shift(t)
        sx, sz = (x + NX - dx) % NX, (z + NZ - dz) % NZ
        return sz // 2, sx * 2 + sz % 2

    barrier = pltpu.get_barrier_semaphore()

    def greet(t, carry):
        pl.semaphore_signal(barrier, inc=1, device_id=target(t)[0], device_id_type=pl.DeviceIdType.MESH)
        return carry

    lax.fori_loop(0, PLANE - 1, greet, 0)
    for other in (sibling, ahead, behind):
        pl.semaphore_signal(barrier, inc=1, device_id=other, device_id_type=pl.DeviceIdType.MESH)
    pl.semaphore_wait(barrier, PLANE + 2)

    def columns(h):
        return pl.ds(pl.multiple_of(h * HD, HD), HD)

    def remote(src, dst, send_sem, recv_sem, device):
        return pltpu.make_async_remote_copy(
            src_ref=src, dst_ref=dst, send_sem=send_sem, recv_sem=recv_sem,
            device_id=device, device_id_type=pl.DeviceIdType.MESH,
        )

    if FLAGS["kv"]:
        def send_kv(t, carry):
            device, h = target(t)
            for which, ref in ((0, k_ref), (1, v_ref)):
                remote(ref.at[:, columns(h)], kv.at[1, my_block, my_sub, which],
                       kv_send.at[which], kv_recv.at[t], device).start()
            return carry

        lax.fori_loop(0, PLANE - 1, send_kv, 0)
        for which, ref in ((0, k_ref), (1, v_ref)):
            pltpu.make_async_copy(ref.at[:, columns(my_head)], kv.at[1, my_block, my_sub, which],
                                  local_sem.at[which]).start()
    if FLAGS["q"]:
        def send_q(t, carry):
            device, h = target(t)
            remote(q_ref.at[:, columns(h)], qbuf.at[my_block // 2, my_sub],
                   q_send, q_recv, device).start()
            return carry

        lax.fori_loop(0, PLANE - 1, send_q, 0)
        pltpu.make_async_copy(q_ref.at[:, columns(my_head)], qbuf.at[my_block // 2, my_sub],
                              local_sem.at[2]).start()

    def chunk(plane, zh, parity, sub):
        return kv.at[plane, 2 * zh + parity, sub]

    if FLAGS["kv"]:
        def pass_on(t, zh, sub):
            here = chunk(1, zh, core, sub)
            remote(here, here, sib_send, sib_recv, sibling).start()
            remote(here, chunk(0, zh, core, sub), fwd_send, fwd_recv.at[t], ahead).start()

        for which, ref in ((0, k_ref), (1, v_ref)):
            pltpu.make_async_copy(ref.at[:, columns(my_head)], kv.at[1, my_block, my_sub, which],
                                  local_sem.at[which]).wait()
        if FLAGS["fwd"]:
            pass_on(PLANE - 1, z // 2, my_sub)

        def take_kv(t, carry):
            zh, sub = source(t)
            here = chunk(1, zh, core, sub)
            remote(here, here, kv_send.at[0], kv_recv.at[t], sibling).wait_recv()
            if FLAGS["fwd"]:
                pass_on(t, zh, sub)
            return carry

        lax.fori_loop(0, PLANE - 1, take_kv, 0)

    if FLAGS["fwd"]:
        def take_prev(t, carry):
            zh, sub = source(t)
            here = chunk(0, zh, core, sub)
            remote(here, here, fwd_send, fwd_recv.at[t], sibling).wait_recv()
            remote(here, here, prev_send, prev_recv, sibling).start()
            return carry

        lax.fori_loop(0, PLANE, take_prev, 0)
        half = kv.at[0, pl.ds(0, OWN)]
        for send, recv in ((sib_send, sib_recv), (prev_send, prev_recv)):
            done = remote(half, half, send, recv, sibling)
            done.wait_send()
            done.wait_recv()
        remote(half, half, fwd_send, sib_recv, sibling).wait_send()

    if FLAGS["kv"]:
        for which, ref in ((0, k_ref), (1, v_ref)):
            most = ref.at[:, pl.ds(0, (PLANE - 1) * HD)]
            remote(most, most, kv_send.at[which], q_recv, sibling).wait_send()
    if FLAGS["q"]:
        pltpu.make_async_copy(q_ref.at[:, columns(my_head)], qbuf.at[my_block // 2, my_sub],
                              local_sem.at[2]).wait()
        most = q_ref.at[:, pl.ds(0, (PLANE - 1) * HD)]
        done = remote(most, most, q_send, q_recv, sibling)
        done.wait_send()
        done.wait_recv()

    row = lax.broadcasted_iota(jnp.int32, (BLOCK, BLOCK), 0)
    col = lax.broadcasted_iota(jnp.int32, (BLOCK, BLOCK), 1)

    def attend(zh, logs):
        i = 2 * zh + core
        first = doc_ref[y * NB + i]
        queries = qbuf[zh].reshape(BLOCK, HD)

        def where(step):
            j = (i + NB - step) % NB
            plane = (j <= i).astype(jnp.int32)
            visible = (y + plane - 1) * NB + j >= first
            return plane, j, visible

        def score(step):
            plane, j, visible = where(step)
            keys = kv[plane, j, :, 0].reshape(BLOCK, HD)
            return lax.dot_general(queries, keys, (((1,), (1,)), ((), ())),
                                   preferred_element_type=jnp.float32), visible

        def fold(s):
            return functools.reduce(jnp.maximum, [s[:, n * HD:(n + 1) * HD] for n in range(BLOCK // HD)])

        home, _ = score(0)
        home = jnp.where(row >= col, home, -jnp.inf)
        scores[0] = home

        def first_pass(step, peak):
            s, visible = score(step)
            scores[step] = s
            return jnp.maximum(peak, jnp.where(visible, fold(s), -jnp.inf))

        peak = lax.fori_loop(1, NB, first_pass, fold(home))
        top = jnp.max(peak, axis=1, keepdims=True)

        def weigh(step, carry):
            total, value = carry
            plane, j, visible = where(step)
            floor = jnp.where(visible, top, jnp.inf)
            w = jnp.exp((scores[step] - floor) * SCALE).astype(jnp.bfloat16)
            wide = w.astype(jnp.float32)
            total = total + functools.reduce(
                jnp.add, [wide[:, n * HD:(n + 1) * HD] for n in range(BLOCK // HD)])
            values = kv[plane, j, :, 1].reshape(BLOCK, HD)
            value = value + jnp.dot(w, values, preferred_element_type=jnp.float32)
            return total, value

        zero = jnp.zeros((BLOCK, HD), jnp.float32)
        total, value = lax.fori_loop(0, NB, weigh, (zero, zero))
        total = jnp.sum(total, axis=1, keepdims=True)
        obuf[zh] = (value / total).astype(jnp.bfloat16).reshape(SUBS, ROWS, HD)
        log_total = top * SCALE + jnp.log(total)
        lane = lax.broadcasted_iota(jnp.int32, (BLOCK, HD), 1)
        logs = jnp.where(lane == zh, log_total, logs)
        if FLAGS["out"]:
            send_out(zh)
        return logs

    def send_out(zh):
        def send(sub, carry):
            tx, tz = sub // 2, 2 * zh + sub % 2
            here = jnp.logical_and(tx == x, tz == z)

            @pl.when(jnp.logical_not(here))
            def _():
                remote(obuf.at[zh, sub], out_ref.at[:, columns(my_head)], o_send, o_recv,
                       chip_device(y, tx, tz, core)).start()

            @pl.when(here)
            def _():
                pltpu.make_async_copy(obuf.at[zh, sub], out_ref.at[:, columns(my_head)],
                                      local_sem.at[3]).start()
            return carry

        lax.fori_loop(0, SUBS, send, 0)

    logs = jnp.zeros((BLOCK, HD), jnp.float32)
    if FLAGS["compute"]:
        logs = lax.fori_loop(0, OWN, attend, logs)
    elif FLAGS["out"]:
        lax.fori_loop(0, OWN, lambda zh, c: (send_out(zh), c)[1], 0)

    if FLAGS["out"]:
        rows = jnp.transpose(logs)
        for zh in range(OWN):
            for n in range(BLOCK // HD):
                lse_stage[zh, n:n + 1, :] = rows[zh:zh + 1, n * HD:(n + 1) * HD]

        def send_logs(zh, carry):
            tz = 2 * zh + z // 4
            here = tz == z

            @pl.when(jnp.logical_not(here))
            def _():
                remote(lse_stage.at[zh], lse_in.at[z % 4], lse_send.at[zh], lse_recv.at[z % 4],
                       chip_device(y, x, tz, core)).start()

            @pl.when(here)
            def _():
                pltpu.make_async_copy(lse_stage.at[zh], lse_in.at[z % 4], local_sem.at[4]).start()
            return carry

        lax.fori_loop(0, OWN, send_logs, 0)

        def take_logs(r, carry):
            sz = (head % 2) * 4 + r
            here = sz == z

            @pl.when(jnp.logical_not(here))
            def _():
                remote(lse_stage.at[0], lse_in.at[r], lse_send.at[0], lse_recv.at[r], sibling).wait_recv()

            @pl.when(here)
            def _():
                pltpu.make_async_copy(lse_stage.at[0], lse_in.at[r], local_sem.at[4]).wait()
            return carry

        lax.fori_loop(0, 4, take_logs, 0)

        def drain_logs(zh, carry):
            @pl.when(2 * zh + z // 4 != z)
            def _():
                remote(lse_stage.at[zh], lse_in.at[0], lse_send.at[zh], lse_recv.at[0], sibling).wait_send()
            return carry

        lax.fori_loop(0, OWN, drain_logs, 0)
        for r in range(4):
            for n in range(BLOCK // HD):
                lse_ref[r:r + 1, n * HD:(n + 1) * HD] = lse_in[r, n:n + 1, :]

        pltpu.make_async_copy(obuf.at[0, 0], out_ref.at[:, columns(my_head)], local_sem.at[3]).wait()
        most = out_ref.at[:, pl.ds(0, (PLANE - 1) * HD)]
        done = remote(most, most, o_send, o_recv, sibling)
        done.wait_send()
        done.wait_recv()


def on_device(query_rows, key_rows, value_rows, doc_first):
    dma = pltpu.SemaphoreType.DMA
    any_space = pl.BlockSpec(memory_space=pl.ANY)
    return pl.pallas_call(
        attend_kernel,
        out_shape=(
            jax.ShapeDtypeStruct((ROWS, PLANE * HD), jnp.bfloat16),
            jax.ShapeDtypeStruct((4, BLOCK), jnp.float32),
        ),
        in_specs=[pl.BlockSpec(memory_space=pltpu.SMEM), any_space, any_space, any_space],
        out_specs=(any_space, pl.BlockSpec(memory_space=pltpu.VMEM)),
        scratch_shapes=[
            pltpu.VMEM((OWN, SUBS, ROWS, HD), jnp.bfloat16),
            pltpu.VMEM((2, NB, SUBS, 2, ROWS, HD), jnp.bfloat16),
            pltpu.VMEM((OWN, SUBS, ROWS, HD), jnp.bfloat16),
            pltpu.VMEM((NB, BLOCK, BLOCK), jnp.float32),
            pltpu.VMEM((OWN, 8, HD), jnp.float32),
            pltpu.VMEM((4, 8, HD), jnp.float32),
            dma((2,)), dma((PLANE,)), dma, dma, dma, dma, dma, dma((PLANE,)),
            dma, dma, dma, dma, dma((4,)), dma((4,)), dma((5,)),
        ],
        compiler_params=pltpu.CompilerParams(
            collective_id=0, has_side_effects=True, vmem_limit_bytes=48 * 1024 * 1024,
        ),
        cost_estimate=pl.CostEstimate(flops=17_000_000_000, bytes_accessed=4_000_000, transcendentals=8_400_000),
    )(doc_first, query_rows, key_rows, value_rows)


def solution(mesh):
    rows = P(("seq", "head"), None)
    return jax.shard_map(
        on_device, mesh=mesh, in_specs=(rows, rows, rows, P()),
        out_specs=(rows, P("head", "seq")), check_vma=False,
    )
```

```python
import functools
import math

import jax
import jax.numpy as jnp
from jax import lax
from jax.experimental import pallas as pl
from jax.experimental.pallas import tpu as pltpu
from jax.sharding import PartitionSpec as P

HD = 128
NX, NY, NZ = 4, 8, 8
PLANE = NX * NZ
ROWS = 64
BLOCK = 512
SUBS = BLOCK // ROWS
NB = 8
OWN = NB // 2
SCALE = 1.0 / math.sqrt(HD)
SCALE2 = SCALE * math.log2(math.e)
TILE = 128
TILES = BLOCK // TILE
PART = 32
FLAGS = {"kv": True, "q": True, "fwd": True, "compute": True, "out": True}


def chip_device(y, x, z, core):
    return ((y * 4 + z // 2) * 2 + core, x * 2 + z % 2)


def shift(t):
    turn = t // 4
    far = 4 - (turn + 1) // 2
    dz = (8 + far * (2 * (turn % 2) - 1)) % 8
    return 3 - t % 4, dz


def attend_kernel(
    doc_ref, q_ref, k_ref, v_ref, out_ref, lse_ref,
    docs, qbuf, kv, obuf, s0, s1, p0, p1, top0, top1, lse_stage, lse_in,
    kv_send, kv_recv, q_send, q_recv, sib_send, sib_recv, fwd_send, fwd_recv,
    prev_send, prev_recv, o_send, o_recv, lse_send, lse_recv, local_sem,
):
    seq = lax.axis_index("seq")
    head = lax.axis_index("head")
    core = seq % 2
    y = seq // 8
    x = head // 2
    z = (seq // 2) % 4 * 2 + head % 2
    my_block = seq % 8
    my_sub = head
    my_head = x * 8 + z

    sibling = chip_device(y, x, z, 1 - core)
    ahead = chip_device((y + 1) % NY, x, z, core)
    behind = chip_device((y + NY - 1) % NY, x, z, core)

    def target(t):
        dx, dz = shift(t)
        tx, tz = (x + dx) % NX, (z + dz) % NZ
        return chip_device(y, tx, tz, core), tx * 8 + tz

    def source(t):
        dx, dz = shift(t)
        sx, sz = (x + NX - dx) % NX, (z + NZ - dz) % NZ
        return sz // 2, sx * 2 + sz % 2

    fetch_docs = pltpu.make_async_copy(doc_ref, docs, local_sem.at[2])
    fetch_docs.start()
    barrier = pltpu.get_barrier_semaphore()

    def greet(t, carry):
        pl.semaphore_signal(barrier, inc=1, device_id=target(t)[0], device_id_type=pl.DeviceIdType.MESH)
        return carry

    lax.fori_loop(0, PLANE - 1, greet, 0)
    for other in (sibling, ahead, behind):
        pl.semaphore_signal(barrier, inc=1, device_id=other, device_id_type=pl.DeviceIdType.MESH)
    pl.semaphore_wait(barrier, PLANE + 2)

    def columns(h):
        return pl.ds(pl.multiple_of(h * HD, HD), HD)

    def remote(src, dst, send_sem, recv_sem, device):
        return pltpu.make_async_remote_copy(
            src_ref=src, dst_ref=dst, send_sem=send_sem, recv_sem=recv_sem,
            device_id=device, device_id_type=pl.DeviceIdType.MESH,
        )

    if FLAGS["kv"]:
        def send_kv(t, carry):
            device, h = target(t)
            for which, ref in ((0, k_ref), (1, v_ref)):
                remote(ref.at[:, columns(h)], kv.at[1, my_block, my_sub, which],
                       kv_send.at[which], kv_recv.at[t], device).start()
            return carry

        lax.fori_loop(0, PLANE - 1, send_kv, 0)
        for which, ref in ((0, k_ref), (1, v_ref)):
            pltpu.make_async_copy(ref.at[:, columns(my_head)], kv.at[1, my_block, my_sub, which],
                                  local_sem.at[which]).start()
    if FLAGS["q"]:
        def send_q(t, carry):
            device, h = target(t)
            remote(q_ref.at[:, columns(h)], qbuf.at[my_block // 2, my_sub],
                   q_send, q_recv.at[my_block // 2], device).start()
            return carry

        lax.fori_loop(0, PLANE - 1, send_q, 0)
        pltpu.make_async_copy(q_ref.at[:, columns(my_head)], qbuf.at[my_block // 2, my_sub],
                              q_recv.at[my_block // 2]).start()

    def chunk(plane, zh, parity, sub):
        return kv.at[plane, 2 * zh + parity, sub]

    if FLAGS["kv"]:
        def pass_on(t, zh, sub):
            here = chunk(1, zh, core, sub)
            remote(here, here, sib_send, sib_recv, sibling).start()
            remote(here, chunk(0, zh, core, sub), fwd_send, fwd_recv.at[t], ahead).start()

        for which, ref in ((0, k_ref), (1, v_ref)):
            pltpu.make_async_copy(ref.at[:, columns(my_head)], kv.at[1, my_block, my_sub, which],
                                  local_sem.at[which]).wait()
        if FLAGS["fwd"]:
            pass_on(PLANE - 1, z // 2, my_sub)

        def take_kv(t, carry):
            zh, sub = source(t)
            here = chunk(1, zh, core, sub)
            remote(here, here, kv_send.at[0], kv_recv.at[t], sibling).wait_recv()
            if FLAGS["fwd"]:
                pass_on(t, zh, sub)
            return carry

        lax.fori_loop(0, PLANE - 1, take_kv, 0)

    if FLAGS["fwd"]:
        def take_prev(t, carry):
            zh, sub = source(t)
            here = chunk(0, zh, core, sub)
            remote(here, here, fwd_send, fwd_recv.at[t], sibling).wait_recv()
            remote(here, here, prev_send, prev_recv, sibling).start()
            return carry

        lax.fori_loop(0, PLANE, take_prev, 0)
        half = kv.at[0, pl.ds(0, OWN)]
        for send, recv in ((sib_send, sib_recv), (prev_send, prev_recv)):
            done = remote(half, half, send, recv, sibling)
            done.wait_send()
            done.wait_recv()
        remote(half, half, fwd_send, sib_recv, sibling).wait_send()

    if FLAGS["kv"]:
        for which, ref in ((0, k_ref), (1, v_ref)):
            most = ref.at[:, pl.ds(0, (PLANE - 1) * HD)]
            remote(most, most, kv_send.at[which], q_send, sibling).wait_send()
    if FLAGS["q"]:
        most = q_ref.at[:, pl.ds(0, (PLANE - 1) * HD)]
        remote(most, most, q_send, q_send, sibling).wait_send()

    def turn(n):
        side = 1 - 2 * (z % 2)
        step = 2 * ((3 - n) // 3) + side * (3 - 2 * n) * (n * (3 - n) // 2)
        return (z // 2 + step + OWN) % OWN

    def place(zh):
        i = 2 * zh + core
        first = docs[y * NB + i]

        def where(step):
            j = (i + NB - step) % NB
            plane = (j <= i).astype(jnp.int32)
            return plane, j, (y + plane - 1) * NB + j >= first

        return where

    def multiply_keys(zh, r, s_ref):
        where = place(zh)
        queries = qbuf[zh, 2 * r:2 * r + 2].reshape(TILE, HD)
        for step in range(NB):
            plane, j, _ = where(step)
            keys = kv[plane, j, :, 0].reshape(BLOCK, HD)
            s_ref[:, step * BLOCK:(step + 1) * BLOCK] = lax.dot_general(
                queries, keys, (((1,), (1,)), ((), ())), preferred_element_type=jnp.float32)

    def weigh(zh, r, s_ref, p_ref, top_ref):
        where = place(zh)
        visible = [where(step)[2] for step in range(NB)]
        for part in range(TILE // PART):
            here = slice(part * PART, (part + 1) * PART)
            row = lax.broadcasted_iota(jnp.int32, (PART, HD), 0) + (r * TILE + part * PART)
            lane = lax.broadcasted_iota(jnp.int32, (PART, HD), 1)
            home, peak = [], None
            for step in range(NB):
                best = None
                for n in range(BLOCK // HD):
                    s = s_ref[here, step * BLOCK + n * HD:step * BLOCK + (n + 1) * HD]
                    if step == 0:
                        s = jnp.where(row >= lane + n * HD, s, -jnp.inf)
                        home.append(s)
                    best = s if best is None else jnp.maximum(best, s)
                if step > 0:
                    best = jnp.where(visible[step], best, -jnp.inf)
                peak = best if peak is None else jnp.maximum(peak, best)
            top = jnp.broadcast_to(jnp.max(peak, axis=1, keepdims=True), (PART, HD))
            top_ref[here, :] = top
            top = top * SCALE2
            for step in range(NB):
                floor = top if step == 0 else jnp.where(visible[step], top, jnp.inf)
                for n in range(BLOCK // HD):
                    columns_here = slice(step * BLOCK + n * HD, step * BLOCK + (n + 1) * HD)
                    s = home[n] if step == 0 else s_ref[here, columns_here]
                    p_ref[here, columns_here] = jnp.exp2(s * SCALE2 - floor).astype(jnp.bfloat16)

    def multiply_values(zh, r, p_ref, top_ref):
        where = place(zh)
        both = jnp.zeros((TILE, 2 * HD), jnp.float32)
        for step in range(NB):
            plane, j, _ = where(step)
            values = kv[plane, j, :, 1].reshape(BLOCK, HD)
            values = jnp.concatenate([values, jnp.ones((BLOCK, HD), jnp.bfloat16)], axis=1)
            both = both + jnp.dot(p_ref[:, step * BLOCK:(step + 1) * BLOCK], values,
                                  preferred_element_type=jnp.float32)
        total = both[:, HD:]
        obuf[zh, 2 * r:2 * r + 2] = (both[:, :HD] / total).astype(jnp.bfloat16).reshape(2, ROWS, HD)
        log_total = top_ref[...] * SCALE + jnp.log(total)
        lse_stage[zh, r:r + 1, :] = jnp.transpose(log_total)[0:1, :]

    def send_out(zh, r):
        for low in range(2):
            sub = 2 * r + low
            tx, tz = r, 2 * zh + low
            here = jnp.logical_and(tx == x, tz == z)

            @pl.when(jnp.logical_not(here))
            def _():
                remote(obuf.at[zh, sub], out_ref.at[:, columns(my_head)], o_send, o_recv,
                       chip_device(y, tx, tz, core)).start()

            @pl.when(here)
            def _():
                pltpu.make_async_copy(obuf.at[zh, sub], out_ref.at[:, columns(my_head)],
                                      local_sem.at[3]).start()

    def take_q(zh):
        block = qbuf.at[zh]
        pltpu.make_async_copy(block, block, q_recv.at[zh]).wait()

    def attend(n, carry):
        now, before, after = turn(n), turn((n + 3) % 4), turn((n + 1) % 4)
        for r in range(TILES):
            s_now, s_next = (s0, s1) if r % 2 == 0 else (s1, s0)
            p_now, p_last = (p0, p1) if r % 2 == 0 else (p1, p0)
            top_now, top_last = (top0, top1) if r % 2 == 0 else (top1, top0)
            if r == TILES - 1:
                @pl.when(n < OWN - 1)
                def _():
                    take_q(after)
                multiply_keys(after, 0, s_next)
            else:
                multiply_keys(now, r + 1, s_next)
            weigh(now, r, s_now, p_now, top_now)
            if r == 0:
                multiply_values(before, TILES - 1, p_last, top_last)

                @pl.when(n > 0)
                def _():
                    send_out(before, TILES - 1)
            else:
                multiply_values(now, r - 1, p_last, top_last)
                send_out(now, r - 1)
        return carry

    fetch_docs.wait()
    take_q(turn(0))
    if FLAGS["compute"]:
        multiply_keys(turn(0), 0, s0)
        lax.fori_loop(0, OWN, attend, 0)
        multiply_values(turn(OWN - 1), TILES - 1, p1, top1)
        send_out(turn(OWN - 1), TILES - 1)
    else:
        for n in range(1, OWN):
            take_q(turn(n))
        for n in range(OWN):
            for r in range(TILES):
                send_out(turn(n), r)

    if FLAGS["out"]:
        def send_logs(zh, carry):
            tz = 2 * zh + z // 4
            here = tz == z

            @pl.when(jnp.logical_not(here))
            def _():
                remote(lse_stage.at[zh], lse_in.at[z % 4], lse_send.at[zh], lse_recv.at[z % 4],
                       chip_device(y, x, tz, core)).start()

            @pl.when(here)
            def _():
                pltpu.make_async_copy(lse_stage.at[zh], lse_in.at[z % 4], local_sem.at[4]).start()
            return carry

        lax.fori_loop(0, OWN, send_logs, 0)

        def take_logs(r, carry):
            sz = (head % 2) * 4 + r
            here = sz == z

            @pl.when(jnp.logical_not(here))
            def _():
                remote(lse_stage.at[0], lse_in.at[r], lse_send.at[0], lse_recv.at[r], sibling).wait_recv()

            @pl.when(here)
            def _():
                pltpu.make_async_copy(lse_stage.at[0], lse_in.at[r], local_sem.at[4]).wait()
            return carry

        lax.fori_loop(0, 4, take_logs, 0)

        def drain_logs(zh, carry):
            @pl.when(2 * zh + z // 4 != z)
            def _():
                remote(lse_stage.at[zh], lse_in.at[0], lse_send.at[zh], lse_recv.at[0], sibling).wait_send()
            return carry

        lax.fori_loop(0, OWN, drain_logs, 0)
        for r in range(4):
            for n in range(BLOCK // HD):
                lse_ref[r:r + 1, n * HD:(n + 1) * HD] = lse_in[r, n:n + 1, :]

        pltpu.make_async_copy(obuf.at[0, 0], out_ref.at[:, columns(my_head)], local_sem.at[3]).wait()
        most = out_ref.at[:, pl.ds(0, (PLANE - 1) * HD)]
        done = remote(most, most, o_send, o_recv, sibling)
        done.wait_send()
        done.wait_recv()


def on_device(query_rows, key_rows, value_rows, doc_first):
    dma = pltpu.SemaphoreType.DMA
    any_space = pl.BlockSpec(memory_space=pl.ANY)
    return pl.pallas_call(
        attend_kernel,
        out_shape=(
            jax.ShapeDtypeStruct((ROWS, PLANE * HD), jnp.bfloat16),
            jax.ShapeDtypeStruct((4, BLOCK), jnp.float32),
        ),
        in_specs=[any_space] * 4,
        out_specs=(any_space, pl.BlockSpec(memory_space=pltpu.VMEM)),
        scratch_shapes=[
            pltpu.SMEM((NB * NY,), jnp.int32),
            pltpu.VMEM((OWN, SUBS, ROWS, HD), jnp.bfloat16),
            pltpu.VMEM((2, NB, SUBS, 2, ROWS, HD), jnp.bfloat16),
            pltpu.VMEM((OWN, SUBS, ROWS, HD), jnp.bfloat16),
            pltpu.VMEM((TILE, NB * BLOCK), jnp.float32),
            pltpu.VMEM((TILE, NB * BLOCK), jnp.float32),
            pltpu.VMEM((TILE, NB * BLOCK), jnp.bfloat16),
            pltpu.VMEM((TILE, NB * BLOCK), jnp.bfloat16),
            pltpu.VMEM((TILE, HD), jnp.float32),
            pltpu.VMEM((TILE, HD), jnp.float32),
            pltpu.VMEM((OWN, 8, HD), jnp.float32),
            pltpu.VMEM((4, 8, HD), jnp.float32),
            dma((2,)), dma((PLANE,)), dma, dma((OWN,)), dma, dma, dma, dma((PLANE,)),
            dma, dma, dma, dma, dma((4,)), dma((4,)), dma((5,)),
        ],
        compiler_params=pltpu.CompilerParams(
            collective_id=0, has_side_effects=True, vmem_limit_bytes=62 * 1024 * 1024,
        ),
        cost_estimate=pl.CostEstimate(flops=17_000_000_000, bytes_accessed=4_000_000, transcendentals=8_400_000),
    )(doc_first, query_rows, key_rows, value_rows)


def solution(mesh):
    rows = P(("seq", "head"), None)
    return jax.shard_map(
        on_device, mesh=mesh, in_specs=(rows, rows, rows, P()),
        out_specs=(rows, P("head", "seq")), check_vma=False,
    )
```

```python
import functools
import math

import jax
import jax.numpy as jnp
from jax import lax
from jax.experimental import pallas as pl
from jax.experimental.pallas import tpu as pltpu
from jax.sharding import PartitionSpec as P

HD = 128
NX, NY, NZ = 4, 8, 8
PLANE = NX * NZ
ROWS = 64
BLOCK = 512
SUBS = BLOCK // ROWS
NB = 8
OWN = NB // 2
SCALE = 1.0 / math.sqrt(HD)
SCALE2 = SCALE * math.log2(math.e)
TILE = 128
TILES = BLOCK // TILE
PART = 32
FLAGS = {"kv": True, "q": True, "fwd": True, "compute": True, "out": True}


def chip_device(y, x, z, core):
    return ((y * 4 + z // 2) * 2 + core, x * 2 + z % 2)


def shift(t):
    turn = t // 4
    far = 4 - (turn + 1) // 2
    dz = (8 + far * (2 * (turn % 2) - 1)) % 8
    return 3 - t % 4, dz


def attend_kernel(
    doc_ref, q_ref, k_ref, v_ref, out_ref, lse_ref,
    docs, qbuf, kv, obuf, s0, s1, p0, p1, top0, top1, lse_stage, lse_in,
    kv_send, kv_recv, q_send, q_recv, sib_send, sib_recv, fwd_send, fwd_recv,
    prev_send, prev_recv, o_send, o_recv, lse_send, lse_recv, local_sem,
):
    seq = lax.axis_index("seq")
    head = lax.axis_index("head")
    core = seq % 2
    y = seq // 8
    x = head // 2
    z = (seq // 2) % 4 * 2 + head % 2
    my_block = seq % 8
    my_sub = head
    my_head = x * 8 + z

    sibling = chip_device(y, x, z, 1 - core)
    ahead = chip_device((y + 1) % NY, x, z, core)
    behind = chip_device((y + NY - 1) % NY, x, z, core)

    def target(t):
        dx, dz = shift(t)
        tx, tz = (x + dx) % NX, (z + dz) % NZ
        return chip_device(y, tx, tz, core), tx * 8 + tz

    def source(t):
        dx, dz = shift(t)
        sx, sz = (x + NX - dx) % NX, (z + NZ - dz) % NZ
        return sz // 2, sx * 2 + sz % 2

    fetch_docs = pltpu.make_async_copy(doc_ref, docs, local_sem.at[2])
    fetch_docs.start()
    barrier = pltpu.get_barrier_semaphore()

    def greet(t, carry):
        pl.semaphore_signal(barrier, inc=1, device_id=target(t)[0], device_id_type=pl.DeviceIdType.MESH)
        return carry

    lax.fori_loop(0, PLANE - 1, greet, 0)
    for other in (sibling, ahead, behind):
        pl.semaphore_signal(barrier, inc=1, device_id=other, device_id_type=pl.DeviceIdType.MESH)
    pl.semaphore_wait(barrier, PLANE + 2)

    def columns(h):
        return pl.ds(pl.multiple_of(h * HD, HD), HD)

    def remote(src, dst, send_sem, recv_sem, device):
        return pltpu.make_async_remote_copy(
            src_ref=src, dst_ref=dst, send_sem=send_sem, recv_sem=recv_sem,
            device_id=device, device_id_type=pl.DeviceIdType.MESH,
        )

    if FLAGS["kv"]:
        def send_kv(step, carry):
            t = PLANE - 2 - step
            device, h = target(t)
            for which, ref in ((0, k_ref), (1, v_ref)):
                remote(ref.at[:, columns(h)], kv.at[1, my_block, my_sub, which],
                       kv_send.at[which], kv_recv.at[t], device).start()
            return carry

        lax.fori_loop(0, PLANE - 1, send_kv, 0)
        for which, ref in ((0, k_ref), (1, v_ref)):
            pltpu.make_async_copy(ref.at[:, columns(my_head)], kv.at[1, my_block, my_sub, which],
                                  local_sem.at[which]).start()
    if FLAGS["q"]:
        def send_q(t, carry):
            device, h = target(t)
            remote(q_ref.at[:, columns(h)], qbuf.at[my_block // 2, my_sub],
                   q_send, q_recv.at[my_block // 2], device).start()
            return carry

        pltpu.make_async_copy(q_ref.at[:, columns(my_head)], qbuf.at[my_block // 2, my_sub],
                              q_recv.at[my_block // 2]).start()

    def chunk(plane, zh, parity, sub):
        return kv.at[plane, 2 * zh + parity, sub]

    if FLAGS["kv"]:
        def pass_on(t, zh, sub):
            here = chunk(1, zh, core, sub)

            @pl.when(zh + core > 0)
            def _():
                remote(here, chunk(0, zh, core, sub), fwd_send, fwd_recv.at[t], ahead).start()

            remote(here, here, sib_send, sib_recv, sibling).start()

        for which, ref in ((0, k_ref), (1, v_ref)):
            pltpu.make_async_copy(ref.at[:, columns(my_head)], kv.at[1, my_block, my_sub, which],
                                  local_sem.at[which]).wait()
        if FLAGS["fwd"]:
            pass_on(PLANE - 1, z // 2, my_sub)

        def take_kv(step, carry):
            t = PLANE - 2 - step
            zh, sub = source(t)
            here = chunk(1, zh, core, sub)
            remote(here, here, kv_send.at[0], kv_recv.at[t], sibling).wait_recv()
            if FLAGS["fwd"]:
                pass_on(t, zh, sub)

            @pl.when(step >= 19)
            def _():
                send_q(step - 19, 0)

            return carry

        lax.fori_loop(0, PLANE - 1, take_kv, 0)
        lax.fori_loop(12, PLANE - 1, send_q, 0)

    if FLAGS["fwd"]:
        def take_prev(step, carry):
            t = PLANE - 1 - step
            zh, sub = source(t)
            here = chunk(0, zh, core, sub)

            @pl.when(zh + core > 0)
            def _():
                remote(here, here, fwd_send, fwd_recv.at[t], sibling).wait_recv()
                remote(here, here, prev_send, prev_recv, sibling).start()

            return carry

        lax.fori_loop(0, PLANE, take_prev, 0)
        half = kv.at[0, pl.ds(0, OWN)]
        done = remote(half, half, sib_send, sib_recv, sibling)
        done.wait_send()
        done.wait_recv()
        for parity in range(2):
            @pl.when(core == parity)
            def _():
                sent = kv.at[0, pl.ds(0, OWN - 1 + parity)]
                remote(sent, sent, fwd_send, prev_recv, sibling).wait_send()
                remote(sent, sent, prev_send, prev_recv, sibling).wait_send()
                got = kv.at[0, pl.ds(0, OWN - parity)]
                remote(got, got, prev_send, prev_recv, sibling).wait_recv()

    if FLAGS["kv"]:
        for which, ref in ((0, k_ref), (1, v_ref)):
            most = ref.at[:, pl.ds(0, (PLANE - 1) * HD)]
            remote(most, most, kv_send.at[which], q_send, sibling).wait_send()
    if FLAGS["q"]:
        most = q_ref.at[:, pl.ds(0, (PLANE - 1) * HD)]
        remote(most, most, q_send, q_send, sibling).wait_send()

    def turn(n):
        side = 1 - 2 * (z % 2)
        step = 2 * ((3 - n) // 3) + side * (3 - 2 * n) * (n * (3 - n) // 2)
        return (z // 2 + step + OWN) % OWN

    def place(zh):
        i = 2 * zh + core
        first = docs[y * NB + i]

        def where(step):
            j = (i + NB - step) % NB
            plane = (j <= i).astype(jnp.int32)
            return plane, j, (y + plane - 1) * NB + j >= first

        return where

    def multiply_keys(zh, r, s_ref):
        where = place(zh)
        queries = qbuf[zh, 2 * r:2 * r + 2].reshape(TILE, HD)
        for step in range(NB):
            plane, j, _ = where(step)
            keys = kv[plane, j, :, 0].reshape(BLOCK, HD)
            s_ref[:, step * BLOCK:(step + 1) * BLOCK] = lax.dot_general(
                queries, keys, (((1,), (1,)), ((), ())), preferred_element_type=jnp.float32)

    def weigh(zh, r, s_ref, p_ref, top_ref):
        where = place(zh)
        visible = [where(step)[2] for step in range(NB)]
        for part in range(TILE // PART):
            here = slice(part * PART, (part + 1) * PART)
            row = lax.broadcasted_iota(jnp.int32, (PART, HD), 0) + (r * TILE + part * PART)
            lane = lax.broadcasted_iota(jnp.int32, (PART, HD), 1)
            home, peak = [], None
            for step in range(NB):
                best = None
                for n in range(BLOCK // HD):
                    s = s_ref[here, step * BLOCK + n * HD:step * BLOCK + (n + 1) * HD]
                    if step == 0:
                        s = jnp.where(row >= lane + n * HD, s, -jnp.inf)
                        home.append(s)
                    best = s if best is None else jnp.maximum(best, s)
                if step > 0:
                    best = jnp.where(visible[step], best, -jnp.inf)
                peak = best if peak is None else jnp.maximum(peak, best)
            top = jnp.broadcast_to(jnp.max(peak, axis=1, keepdims=True), (PART, HD))
            top_ref[here, :] = top
            top = top * SCALE2
            for step in range(NB):
                floor = top if step == 0 else jnp.where(visible[step], top, jnp.inf)
                for n in range(BLOCK // HD):
                    columns_here = slice(step * BLOCK + n * HD, step * BLOCK + (n + 1) * HD)
                    s = home[n] if step == 0 else s_ref[here, columns_here]
                    p_ref[here, columns_here] = jnp.exp2(s * SCALE2 - floor).astype(jnp.bfloat16)

    def multiply_values(zh, r, p_ref, top_ref):
        where = place(zh)
        both = jnp.zeros((TILE, 2 * HD), jnp.float32)
        for step in range(NB):
            plane, j, _ = where(step)
            values = kv[plane, j, :, 1].reshape(BLOCK, HD)
            values = jnp.concatenate([values, jnp.ones((BLOCK, HD), jnp.bfloat16)], axis=1)
            both = both + jnp.dot(p_ref[:, step * BLOCK:(step + 1) * BLOCK], values,
                                  preferred_element_type=jnp.float32)
        total = both[:, HD:]
        obuf[zh, 2 * r:2 * r + 2] = (both[:, :HD] / total).astype(jnp.bfloat16).reshape(2, ROWS, HD)
        log_total = top_ref[...] * SCALE + jnp.log(total)
        lse_stage[zh, r:r + 1, :] = jnp.transpose(log_total)[0:1, :]

    def send_out(zh):
        for r in range(TILES):
            for low in range(2):
                source = obuf.at[zh, 2 * r + low]
                to = out_ref.at[:, columns(my_head)]
                device = (y * NB + 2 * zh + core, 2 * r + low)
                mine = jnp.logical_and(zh == z // 2, head == 2 * r + low)

                @pl.when(jnp.logical_not(mine))
                def _():
                    remote(source, to, o_send, o_recv, device).start()

                @pl.when(mine)
                def _():
                    pltpu.make_async_copy(source, to, local_sem.at[3]).start()

    def take_q(zh):
        block = qbuf.at[zh]
        pltpu.make_async_copy(block, block, q_recv.at[zh]).wait()

    def attend(n, carry):
        now, before, after = turn(n), turn((n + 3) % 4), turn((n + 1) % 4)
        for r in range(TILES):
            s_now, s_next = (s0, s1) if r % 2 == 0 else (s1, s0)
            p_now, p_last = (p0, p1) if r % 2 == 0 else (p1, p0)
            top_now, top_last = (top0, top1) if r % 2 == 0 else (top1, top0)
            if r == TILES - 1:
                @pl.when(n < OWN - 1)
                def _():
                    take_q(after)
                multiply_keys(after, 0, s_next)
            else:
                multiply_keys(now, r + 1, s_next)
            weigh(now, r, s_now, p_now, top_now)
            if r == 0:
                multiply_values(before, TILES - 1, p_last, top_last)

                @pl.when(n > 0)
                def _():
                    send_out(before)
            else:
                multiply_values(now, r - 1, p_last, top_last)
        return carry

    fetch_docs.wait()
    take_q(turn(0))
    if FLAGS["compute"]:
        multiply_keys(turn(0), 0, s0)
        lax.fori_loop(0, OWN, attend, 0)
        multiply_values(turn(OWN - 1), TILES - 1, p1, top1)
        send_out(turn(OWN - 1))
    else:
        for n in range(1, OWN):
            take_q(turn(n))
        for n in range(OWN):
            send_out(turn(n))

    if FLAGS["out"]:
        def send_logs(zh, carry):
            tz = 2 * zh + z // 4
            here = tz == z

            @pl.when(jnp.logical_not(here))
            def _():
                remote(lse_stage.at[zh], lse_in.at[z % 4], lse_send.at[zh], lse_recv.at[z % 4],
                       chip_device(y, x, tz, core)).start()

            @pl.when(here)
            def _():
                pltpu.make_async_copy(lse_stage.at[zh], lse_in.at[z % 4], local_sem.at[4]).start()
            return carry

        lax.fori_loop(0, OWN, send_logs, 0)

        def take_logs(r, carry):
            sz = (head % 2) * 4 + r
            here = sz == z

            @pl.when(jnp.logical_not(here))
            def _():
                remote(lse_stage.at[0], lse_in.at[r], lse_send.at[0], lse_recv.at[r], sibling).wait_recv()

            @pl.when(here)
            def _():
                pltpu.make_async_copy(lse_stage.at[0], lse_in.at[r], local_sem.at[4]).wait()
            return carry

        lax.fori_loop(0, 4, take_logs, 0)

        def drain_logs(zh, carry):
            @pl.when(2 * zh + z // 4 != z)
            def _():
                remote(lse_stage.at[zh], lse_in.at[0], lse_send.at[zh], lse_recv.at[0], sibling).wait_send()
            return carry

        lax.fori_loop(0, OWN, drain_logs, 0)
        for r in range(4):
            for n in range(BLOCK // HD):
                lse_ref[r:r + 1, n * HD:(n + 1) * HD] = lse_in[r, n:n + 1, :]

        pltpu.make_async_copy(obuf.at[0, 0], out_ref.at[:, columns(my_head)], local_sem.at[3]).wait()
        most = out_ref.at[:, pl.ds(0, (PLANE - 1) * HD)]
        done = remote(most, most, o_send, o_recv, sibling)
        done.wait_send()
        done.wait_recv()


def on_device(query_rows, key_rows, value_rows, doc_first):
    dma = pltpu.SemaphoreType.DMA
    any_space = pl.BlockSpec(memory_space=pl.ANY)
    return pl.pallas_call(
        attend_kernel,
        out_shape=(
            jax.ShapeDtypeStruct((ROWS, PLANE * HD), jnp.bfloat16),
            jax.ShapeDtypeStruct((4, BLOCK), jnp.float32),
        ),
        in_specs=[any_space] * 4,
        out_specs=(any_space, pl.BlockSpec(memory_space=pltpu.VMEM)),
        scratch_shapes=[
            pltpu.SMEM((NB * NY,), jnp.int32),
            pltpu.VMEM((OWN, SUBS, ROWS, HD), jnp.bfloat16),
            pltpu.VMEM((2, NB, SUBS, 2, ROWS, HD), jnp.bfloat16),
            pltpu.VMEM((OWN, SUBS, ROWS, HD), jnp.bfloat16),
            pltpu.VMEM((TILE, NB * BLOCK), jnp.float32),
            pltpu.VMEM((TILE, NB * BLOCK), jnp.float32),
            pltpu.VMEM((TILE, NB * BLOCK), jnp.bfloat16),
            pltpu.VMEM((TILE, NB * BLOCK), jnp.bfloat16),
            pltpu.VMEM((TILE, HD), jnp.float32),
            pltpu.VMEM((TILE, HD), jnp.float32),
            pltpu.VMEM((OWN, 8, HD), jnp.float32),
            pltpu.VMEM((4, 8, HD), jnp.float32),
            dma((2,)), dma((PLANE,)), dma, dma((OWN,)), dma, dma, dma, dma((PLANE,)),
            dma, dma, dma, dma, dma((4,)), dma((4,)), dma((5,)),
        ],
        compiler_params=pltpu.CompilerParams(
            collective_id=0, has_side_effects=True, vmem_limit_bytes=62 * 1024 * 1024,
        ),
        cost_estimate=pl.CostEstimate(flops=17_000_000_000, bytes_accessed=4_000_000, transcendentals=8_400_000),
    )(doc_first, query_rows, key_rows, value_rows)


def solution(mesh):
    rows = P(("seq", "head"), None)
    return jax.shard_map(
        on_device, mesh=mesh, in_specs=(rows, rows, rows, P()),
        out_specs=(rows, P("head", "seq")), check_vma=False,
    )
```

```python
import functools
import math

import jax
import jax.numpy as jnp
from jax import lax
from jax.experimental import pallas as pl
from jax.experimental.pallas import tpu as pltpu
from jax.sharding import PartitionSpec as P

HD = 128
NX, NY, NZ = 4, 8, 8
PLANE = NX * NZ
ROWS = 64
BLOCK = 512
SUBS = BLOCK // ROWS
NB = 8
OWN = NB // 2
SCALE = 1.0 / math.sqrt(HD)
SCALE2 = SCALE * math.log2(math.e)
TILE = 128
TILES = BLOCK // TILE
PART = 32
FLAGS = {"kv": True, "q": True, "fwd": True, "compute": True, "out": True}


def chip_device(y, x, z, core):
    return ((y * 4 + z // 2) * 2 + core, x * 2 + z % 2)


def shift(t):
    turn = t // 4
    far = 4 - (turn + 1) // 2
    dz = (8 + far * (2 * (turn % 2) - 1)) % 8
    return 3 - t % 4, dz


def attend_kernel(
    doc_ref, q_ref, k_ref, v_ref, out_ref, lse_ref,
    docs, qbuf, kv, obuf, s0, s1, p0, p1, top0, top1, lse_stage, lse_in,
    kv_send, kv_recv, q_send, q_recv, sib_send, sib_recv, fwd_send, fwd_recv,
    prev_send, prev_recv, o_send, o_recv, lse_send, lse_recv, local_sem,
):
    seq = lax.axis_index("seq")
    head = lax.axis_index("head")
    core = seq % 2
    y = seq // 8
    x = head // 2
    z = (seq // 2) % 4 * 2 + head % 2
    my_block = seq % 8
    my_sub = head
    my_head = x * 8 + z

    sibling = chip_device(y, x, z, 1 - core)
    ahead = chip_device((y + 1) % NY, x, z, core)
    behind = chip_device((y + NY - 1) % NY, x, z, core)

    def target(t):
        dx, dz = shift(t)
        tx, tz = (x + dx) % NX, (z + dz) % NZ
        return chip_device(y, tx, tz, core), tx * 8 + tz

    def source(t):
        dx, dz = shift(t)
        sx, sz = (x + NX - dx) % NX, (z + NZ - dz) % NZ
        return sz // 2, sx * 2 + sz % 2

    fetch_docs = pltpu.make_async_copy(doc_ref, docs, local_sem.at[2])
    fetch_docs.start()
    barrier = pltpu.get_barrier_semaphore()

    def greet(t, carry):
        pl.semaphore_signal(barrier, inc=1, device_id=target(t)[0], device_id_type=pl.DeviceIdType.MESH)
        return carry

    lax.fori_loop(0, PLANE - 1, greet, 0)
    for other in (sibling, ahead, behind):
        pl.semaphore_signal(barrier, inc=1, device_id=other, device_id_type=pl.DeviceIdType.MESH)
    pl.semaphore_wait(barrier, PLANE + 2)

    def columns(h):
        return pl.ds(pl.multiple_of(h * HD, HD), HD)

    def remote(src, dst, send_sem, recv_sem, device):
        return pltpu.make_async_remote_copy(
            src_ref=src, dst_ref=dst, send_sem=send_sem, recv_sem=recv_sem,
            device_id=device, device_id_type=pl.DeviceIdType.MESH,
        )

    if FLAGS["kv"]:
        def send_kv(step, carry):
            t = PLANE - 2 - step
            device, h = target(t)
            for which, ref in ((0, k_ref), (1, v_ref)):
                remote(ref.at[:, columns(h)], kv.at[1, my_block, my_sub, which],
                       kv_send.at[which], kv_recv.at[t], device).start()
            return carry

        lax.fori_loop(0, PLANE - 1, send_kv, 0)
        for which, ref in ((0, k_ref), (1, v_ref)):
            pltpu.make_async_copy(ref.at[:, columns(my_head)], kv.at[1, my_block, my_sub, which],
                                  local_sem.at[which]).start()
    if FLAGS["q"]:
        def send_q(t, carry):
            device, h = target(t)
            remote(q_ref.at[:, columns(h)], qbuf.at[my_block // 2, my_sub],
                   q_send, q_recv.at[my_block // 2], device).start()
            return carry

        pltpu.make_async_copy(q_ref.at[:, columns(my_head)], qbuf.at[my_block // 2, my_sub],
                              q_recv.at[my_block // 2]).start()

    def chunk(plane, zh, parity, sub):
        return kv.at[plane, 2 * zh + parity, sub]

    if FLAGS["kv"]:
        def pass_on(t, zh, sub):
            here = chunk(1, zh, core, sub)

            @pl.when(zh + core > 0)
            def _():
                remote(here, chunk(0, zh, core, sub), fwd_send, fwd_recv.at[t], ahead).start()

            remote(here, here, sib_send, sib_recv, sibling).start()

        for which, ref in ((0, k_ref), (1, v_ref)):
            pltpu.make_async_copy(ref.at[:, columns(my_head)], kv.at[1, my_block, my_sub, which],
                                  local_sem.at[which]).wait()
        if FLAGS["fwd"]:
            pass_on(PLANE - 1, z // 2, my_sub)

        def take_kv(step, carry):
            t = PLANE - 2 - step
            zh, sub = source(t)
            here = chunk(1, zh, core, sub)
            remote(here, here, kv_send.at[0], kv_recv.at[t], sibling).wait_recv()
            if FLAGS["fwd"]:
                pass_on(t, zh, sub)

            @pl.when(step >= 19)
            def _():
                send_q(step - 19, 0)

            return carry

        lax.fori_loop(0, PLANE - 1, take_kv, 0)
        lax.fori_loop(12, PLANE - 1, send_q, 0)

    if FLAGS["fwd"]:
        def take_prev(step, carry):
            t = PLANE - 1 - step
            zh, sub = source(t)
            here = chunk(0, zh, core, sub)

            @pl.when(zh + core > 0)
            def _():
                remote(here, here, fwd_send, fwd_recv.at[t], sibling).wait_recv()
                remote(here, here, prev_send, prev_recv, sibling).start()

            return carry

        lax.fori_loop(0, PLANE, take_prev, 0)
        half = kv.at[0, pl.ds(0, OWN)]
        done = remote(half, half, sib_send, sib_recv, sibling)
        done.wait_send()
        done.wait_recv()
        for parity in range(2):
            @pl.when(core == parity)
            def _():
                sent = kv.at[0, pl.ds(0, OWN - 1 + parity)]
                remote(sent, sent, fwd_send, prev_recv, sibling).wait_send()
                remote(sent, sent, prev_send, prev_recv, sibling).wait_send()
                got = kv.at[0, pl.ds(0, OWN - parity)]
                remote(got, got, prev_send, prev_recv, sibling).wait_recv()

    if FLAGS["kv"]:
        for which, ref in ((0, k_ref), (1, v_ref)):
            most = ref.at[:, pl.ds(0, (PLANE - 1) * HD)]
            remote(most, most, kv_send.at[which], q_send, sibling).wait_send()
    if FLAGS["q"]:
        most = q_ref.at[:, pl.ds(0, (PLANE - 1) * HD)]
        remote(most, most, q_send, q_send, sibling).wait_send()

    def turn(n):
        side = 1 - 2 * (z % 2)
        step = 2 * ((3 - n) // 3) + side * (3 - 2 * n) * (n * (3 - n) // 2)
        return (z // 2 + step + OWN) % OWN

    def place(zh):
        i = 2 * zh + core
        first = docs[y * NB + i]

        def where(step):
            j = (i + NB - step) % NB
            plane = (j <= i).astype(jnp.int32)
            return plane, j, (y + plane - 1) * NB + j >= first

        return where

    def multiply_keys(zh, r, s_ref):
        where = place(zh)
        queries = qbuf[zh, 2 * r:2 * r + 2].reshape(TILE, HD)
        for step in range(NB):
            plane, j, _ = where(step)
            keys = kv[plane, j, :, 0].reshape(BLOCK, HD)
            s_ref[:, step * BLOCK:(step + 1) * BLOCK] = lax.dot_general(
                queries, keys, (((1,), (1,)), ((), ())), preferred_element_type=jnp.float32)

    def weigh(zh, r, s_ref, p_ref, top_ref):
        where = place(zh)
        visible = [where(step)[2] for step in range(NB)]
        for part in range(TILE // PART):
            here = slice(part * PART, (part + 1) * PART)
            row = lax.broadcasted_iota(jnp.int32, (PART, HD), 0) + (r * TILE + part * PART)
            lane = lax.broadcasted_iota(jnp.int32, (PART, HD), 1)
            home, peak = [], None
            for step in range(NB):
                best = None
                for n in range(BLOCK // HD):
                    s = s_ref[here, step * BLOCK + n * HD:step * BLOCK + (n + 1) * HD]
                    if step == 0:
                        s = jnp.where(row >= lane + n * HD, s, -jnp.inf)
                        home.append(s)
                    best = s if best is None else jnp.maximum(best, s)
                if step > 0:
                    best = jnp.where(visible[step], best, -jnp.inf)
                peak = best if peak is None else jnp.maximum(peak, best)
            top = jnp.broadcast_to(jnp.max(peak, axis=1, keepdims=True), (PART, HD))
            top_ref[here, :] = top
            top = top * SCALE2
            for step in range(NB):
                floor = top if step == 0 else jnp.where(visible[step], top, jnp.inf)
                for n in range(BLOCK // HD):
                    columns_here = slice(step * BLOCK + n * HD, step * BLOCK + (n + 1) * HD)
                    s = home[n] if step == 0 else s_ref[here, columns_here]
                    p_ref[here, columns_here] = jnp.exp2(s * SCALE2 - floor).astype(jnp.bfloat16)

    def multiply_values(zh, r, p_ref, top_ref):
        where = place(zh)
        both = jnp.zeros((TILE, 2 * HD), jnp.float32)
        for step in range(NB):
            plane, j, _ = where(step)
            values = kv[plane, j, :, 1].reshape(BLOCK, HD)
            values = jnp.concatenate([values, jnp.ones((BLOCK, HD), jnp.bfloat16)], axis=1)
            both = both + jnp.dot(p_ref[:, step * BLOCK:(step + 1) * BLOCK], values,
                                  preferred_element_type=jnp.float32)
        total = both[:, HD:]
        obuf[zh, 2 * r:2 * r + 2] = (both[:, :HD] / total).astype(jnp.bfloat16).reshape(2, ROWS, HD)
        log_total = top_ref[...] * SCALE + jnp.log(total)
        lse_stage[zh, r:r + 1, :] = jnp.transpose(log_total)[0:1, :]

    def send_out(zh, tiles):
        for r in tiles:
            for low in range(2):
                source = obuf.at[zh, 2 * r + low]
                to = out_ref.at[:, columns(my_head)]
                device = (y * NB + 2 * zh + core, 2 * r + low)
                mine = jnp.logical_and(zh == z // 2, head == 2 * r + low)

                @pl.when(jnp.logical_not(mine))
                def _():
                    remote(source, to, o_send, o_recv, device).start()

                @pl.when(mine)
                def _():
                    pltpu.make_async_copy(source, to, local_sem.at[3]).start()

    def take_q(zh):
        block = qbuf.at[zh]
        pltpu.make_async_copy(block, block, q_recv.at[zh]).wait()

    def attend(n, carry):
        now, before, after = turn(n), turn((n + 3) % 4), turn((n + 1) % 4)
        for r in range(TILES):
            s_now, s_next = (s0, s1) if r % 2 == 0 else (s1, s0)
            p_now, p_last = (p0, p1) if r % 2 == 0 else (p1, p0)
            top_now, top_last = (top0, top1) if r % 2 == 0 else (top1, top0)
            if r == TILES - 1:
                @pl.when(n < OWN - 1)
                def _():
                    take_q(after)
                multiply_keys(after, 0, s_next)
            else:
                multiply_keys(now, r + 1, s_next)
            weigh(now, r, s_now, p_now, top_now)
            if r == 0:
                multiply_values(before, TILES - 1, p_last, top_last)

                @pl.when(n > 0)
                def _():
                    send_out(before, (2, 3))
            else:
                multiply_values(now, r - 1, p_last, top_last)
                if r == 2:
                    send_out(now, (0, 1))
        return carry

    fetch_docs.wait()
    take_q(turn(0))
    if FLAGS["compute"]:
        multiply_keys(turn(0), 0, s0)
        lax.fori_loop(0, OWN, attend, 0)
        multiply_values(turn(OWN - 1), TILES - 1, p1, top1)
        send_out(turn(OWN - 1), (2, 3))
    else:
        for n in range(1, OWN):
            take_q(turn(n))
        for n in range(OWN):
            send_out(turn(n), range(TILES))

    if FLAGS["out"]:
        def send_logs(zh, carry):
            tz = 2 * zh + z // 4
            here = tz == z

            @pl.when(jnp.logical_not(here))
            def _():
                remote(lse_stage.at[zh], lse_in.at[z % 4], lse_send.at[zh], lse_recv.at[z % 4],
                       chip_device(y, x, tz, core)).start()

            @pl.when(here)
            def _():
                pltpu.make_async_copy(lse_stage.at[zh], lse_in.at[z % 4], local_sem.at[4]).start()
            return carry

        lax.fori_loop(0, OWN, send_logs, 0)

        def take_logs(r, carry):
            sz = (head % 2) * 4 + r
            here = sz == z

            @pl.when(jnp.logical_not(here))
            def _():
                remote(lse_stage.at[0], lse_in.at[r], lse_send.at[0], lse_recv.at[r], sibling).wait_recv()

            @pl.when(here)
            def _():
                pltpu.make_async_copy(lse_stage.at[0], lse_in.at[r], local_sem.at[4]).wait()
            return carry

        lax.fori_loop(0, 4, take_logs, 0)

        def drain_logs(zh, carry):
            @pl.when(2 * zh + z // 4 != z)
            def _():
                remote(lse_stage.at[zh], lse_in.at[0], lse_send.at[zh], lse_recv.at[0], sibling).wait_send()
            return carry

        lax.fori_loop(0, OWN, drain_logs, 0)
        for r in range(4):
            for n in range(BLOCK // HD):
                lse_ref[r:r + 1, n * HD:(n + 1) * HD] = lse_in[r, n:n + 1, :]

        pltpu.make_async_copy(obuf.at[0, 0], out_ref.at[:, columns(my_head)], local_sem.at[3]).wait()
        most = out_ref.at[:, pl.ds(0, (PLANE - 1) * HD)]
        done = remote(most, most, o_send, o_recv, sibling)
        done.wait_send()
        done.wait_recv()


def on_device(query_rows, key_rows, value_rows, doc_first):
    dma = pltpu.SemaphoreType.DMA
    any_space = pl.BlockSpec(memory_space=pl.ANY)
    return pl.pallas_call(
        attend_kernel,
        out_shape=(
            jax.ShapeDtypeStruct((ROWS, PLANE * HD), jnp.bfloat16),
            jax.ShapeDtypeStruct((4, BLOCK), jnp.float32),
        ),
        in_specs=[any_space] * 4,
        out_specs=(any_space, pl.BlockSpec(memory_space=pltpu.VMEM)),
        scratch_shapes=[
            pltpu.SMEM((NB * NY,), jnp.int32),
            pltpu.VMEM((OWN, SUBS, ROWS, HD), jnp.bfloat16),
            pltpu.VMEM((2, NB, SUBS, 2, ROWS, HD), jnp.bfloat16),
            pltpu.VMEM((OWN, SUBS, ROWS, HD), jnp.bfloat16),
            pltpu.VMEM((TILE, NB * BLOCK), jnp.float32),
            pltpu.VMEM((TILE, NB * BLOCK), jnp.float32),
            pltpu.VMEM((TILE, NB * BLOCK), jnp.bfloat16),
            pltpu.VMEM((TILE, NB * BLOCK), jnp.bfloat16),
            pltpu.VMEM((TILE, HD), jnp.float32),
            pltpu.VMEM((TILE, HD), jnp.float32),
            pltpu.VMEM((OWN, 8, HD), jnp.float32),
            pltpu.VMEM((4, 8, HD), jnp.float32),
            dma((2,)), dma((PLANE,)), dma, dma((OWN,)), dma, dma, dma, dma((PLANE,)),
            dma, dma, dma, dma, dma((4,)), dma((4,)), dma((5,)),
        ],
        compiler_params=pltpu.CompilerParams(
            collective_id=0, has_side_effects=True, vmem_limit_bytes=62 * 1024 * 1024,
        ),
        cost_estimate=pl.CostEstimate(flops=17_000_000_000, bytes_accessed=4_000_000, transcendentals=8_400_000),
    )(doc_first, query_rows, key_rows, value_rows)


def solution(mesh):
    rows = P(("seq", "head"), None)
    return jax.shard_map(
        on_device, mesh=mesh, in_specs=(rows, rows, rows, P()),
        out_specs=(rows, P("head", "seq")), check_vma=False,
    )
```
